32 devices in a mesh: dp: 16 (over z, y, x), tensor: 2 (over core).
Axes of the slice: x: 2, y: 2, z: 4, core: 2. Of those that a mesh axis runs over, the one named last changes fastest.
Arguments:
- hidden: bfloat16 [2048, 5120], P('dp', 'tensor'), may hold values from -6 to 6
- queries: bfloat16 [2048, 8192], P('dp', 'tensor'), may hold values from -21 to 21
- out_grad: bfloat16 [2048, 8192], P('dp', 'tensor'), may hold values from -16 to 16
- w_key: bfloat16 [5120, 1024], P(None, 'tensor'), may hold values from -0.078125 to 0.078125
- w_value: bfloat16 [5120, 1024], P(None, 'tensor'), may hold values from -0.078125 to 0.078125
- prompt_kv: bfloat16 [16, 2, 1024, 1024], P('dp', None, None, 'tensor'), may hold values from -6 to 6
- block_dest: int32 [16], replicated, may hold values from 0 to 15, as said below
- resp_len: int32 [16], replicated, may hold values from 1 to 128, as said below
Outputs:
- grad_query: bfloat16 [2048, 8192], P('dp', 'tensor')
- grad_hidden: bfloat16 [2048, 5120], P('dp', 'tensor')
- grad_prompt_kv: bfloat16 [16, 2, 1024, 1024], P('dp', None, None, 'tensor')
The draws below stay inside these ranges and needn't reach their ends.
Inputs may be any that keep to these rules, and one draw needn't show every extreme that they name: block_dest[b] // 4 == b // 4; no shard is the destination of more than 3 blocks, and in every draw some shard is the destination of exactly 3. `resp_len`: some block is full in every draw.
All inputs are finite; a program needn't handle non-finite values.
Results may differ from the reference program's by a relative error of at most 0.019.
Values may be sent and summed in bfloat16 or wider, within the bound.
No kernel may reach another device: no remote copies, remote signals or barrier semaphores. Data moves between devices by JAX's collectives and lax.ppermute only.
A program may use at most 128 MiB of HBM per device.

```python
import math
import jax
import jax.numpy as jnp
from jax import lax

D = 5120
HQ = 64
KVH = 8
HD = 128
PL = 1024
BT = 128
GROUP = 4
CAP = 3
NB = 16


def shard_routes(key):
    groups = NB // GROUP
    group_keys = jax.random.split(jax.random.fold_in(key, 11), groups)
    shuffled = jax.vmap(lambda one_key: jax.random.permutation(one_key, GROUP))(group_keys)
    counts = jax.random.randint(jax.random.fold_in(key, 12), (groups,), 1, CAP + 1)
    chosen = jax.random.randint(jax.random.fold_in(key, 13), (), 0, groups - 1)
    counts = jnp.where(jnp.arange(groups) == chosen, CAP, counts)
    rank_local = jnp.argsort(shuffled, axis=1)
    hot_shard = shuffled[:, :1]
    local_ids = jnp.arange(GROUP)[None, :]
    dest_local = jnp.where(rank_local < counts[:, None], hot_shard, local_ids)
    last_pattern = jnp.array([0, GROUP - 1, GROUP - 1, 0], jnp.int32)[None, :]
    is_last = (jnp.arange(groups) == groups - 1)[:, None]
    dest_local = jnp.where(is_last, last_pattern, dest_local)
    middle_group = NB // 2 // GROUP
    upper_pattern = jnp.array([0, 0, 0, GROUP - 1], jnp.int32)[None, :]
    lower_pattern = jnp.array([0, 1, 2, 0], jnp.int32)[None, :]
    is_upper = (jnp.arange(groups) == middle_group)[:, None]
    is_lower = (jnp.arange(groups) == middle_group - 1)[:, None]
    dest_local = jnp.where(is_upper, upper_pattern, dest_local)
    dest_local = jnp.where(is_lower, lower_pattern, dest_local)
    return (dest_local + jnp.arange(groups)[:, None] * GROUP).reshape(NB).astype(jnp.int32)


def draw_block_dest(key, part):
    return shard_routes(key)


def draw_resp_len(key, part):
    key = jax.random.fold_in(key, 2)
    lengths = jax.random.randint(jax.random.fold_in(key, 1), (NB,), 1, BT + 1)
    chosen = jax.random.randint(jax.random.fold_in(key, 2), (), 0, NB)
    return jnp.where(jnp.arange(NB) == chosen, BT, lengths).astype(jnp.int32)


def draw_prompt_kv(key, part):
    key = jax.random.fold_in(key, 3)
    draw_dims = (NB, 2, PL, KVH * HD)
    base_draw = jax.random.truncated_normal(key, -6.0, 6.0, draw_dims, jnp.float32)
    return base_draw.astype(jnp.bfloat16)


def draw_queries(key, part):
    key = jax.random.fold_in(key, 4)
    draw_dims = (NB * BT, HQ * HD)
    base_draw = jax.random.truncated_normal(key, -6.0, 6.0, draw_dims, jnp.float32)
    return base_draw.astype(jnp.bfloat16)


def block_levels(stream_key, shape, cuts, least, high):
    factor_of, own = 1.0, jax.random.fold_in(stream_key, 6)
    for axis_at, shards_of in cuts:
        draws = jnp.exp(jax.random.uniform(jax.random.fold_in(own, axis_at), (shards_of,), jnp.float32, least / len(cuts), high / len(cuts)))
        factor_of = factor_of * jnp.repeat(draws, shape[axis_at] // shards_of).reshape([-1 if axis == axis_at else 1 for axis in range(len(shape))])
    return factor_of


def bell_draw(own_key, extent, deviation, limit, pieces=(), held_as=jnp.bfloat16):
    result = jax.random.normal(own_key, extent, jnp.float32) * deviation
    if len(pieces) > 0:
        result = block_levels(own_key, extent, pieces, -0.22, 0.18) * result
    return jnp.clip(result, min=-limit, max=limit).astype(held_as)


def setup_inputs(seed: int = 0) -> dict:
    key_of = jax.random.split(jax.random.key(seed), 9)
    return {
        "hidden": bell_draw(key_of[0], (NB * BT, D), 1.0, 6.0, ((0, 16), (1, 2))),
        "queries": draw_queries(jax.random.fold_in(key_of[8], 71), 0),
        "out_grad": bell_draw(key_of[2], (NB * BT, HQ * HD), 4.0, 16.0, ((0, 16), (1, 2))),
        "w_key": bell_draw(key_of[3], (D, KVH * HD), D ** -0.5, 0.078125, ((1, 2),)),
        "w_value": bell_draw(key_of[4], (D, KVH * HD), D ** -0.5, 0.078125, ((1, 2),)),
        "prompt_kv": draw_prompt_kv(jax.random.fold_in(key_of[8], 71), 0),
        "block_dest": draw_block_dest(jax.random.fold_in(key_of[8], 71), 0),
        "resp_len": draw_resp_len(jax.random.fold_in(key_of[8], 71), 0),
    }


big_negative = -1e+30

def one_block(inputs, w_key, w_value):
    block_hidden, block_query, block_upstream, prompt_pair, length = inputs
    group_size = HQ // KVH
    key_count = PL + BT
    resp_keys = jnp.dot(block_hidden, w_key, preferred_element_type=jnp.float32).astype(jnp.bfloat16)
    resp_values = jnp.dot(block_hidden, w_value, preferred_element_type=jnp.float32).astype(jnp.bfloat16)
    all_keys = jnp.concatenate([prompt_pair[0], resp_keys], axis=0)
    all_values = jnp.concatenate([prompt_pair[1], resp_values], axis=0)
    row_pos = lax.broadcasted_iota(jnp.int32, (BT, key_count), 0)
    col_pos = lax.broadcasted_iota(jnp.int32, (BT, key_count), 1) - PL
    visible = (col_pos < 0) | (col_pos <= row_pos) & (col_pos < length)
    query_full = block_query.astype(jnp.float32).reshape(BT, KVH, group_size, HD)
    keys_full = all_keys.astype(jnp.float32).reshape(key_count, KVH, HD)
    values_full = all_values.astype(jnp.float32).reshape(key_count, KVH, HD)
    live_rows = lax.broadcasted_iota(jnp.int32, (BT, 1, 1, 1), 0) < length
    upstream = jnp.where(live_rows, block_upstream.reshape(BT, KVH, group_size, HD), jnp.zeros((), jnp.bfloat16)).astype(jnp.float32)
    score_scale = 1.0 / math.sqrt(HD)
    scores = jnp.einsum('ikgd,jkd->kgij', query_full, keys_full) * score_scale
    scores = jnp.where(visible, scores, big_negative)
    row_peak = lax.optimization_barrier(jnp.max(scores, axis=3, keepdims=True))
    exponent = jnp.exp(scores - row_peak)
    softmax_out = exponent / lax.optimization_barrier(jnp.sum(exponent, axis=3, keepdims=True))
    weights = lax.optimization_barrier(softmax_out.astype(jnp.bfloat16)).astype(jnp.float32)
    attended = jnp.einsum('kgij,jkd->ikgd', weights, values_full)
    row_dot = lax.optimization_barrier(jnp.sum(upstream * attended, axis=3))
    prob_grad = jnp.einsum('ikgd,jkd->kgij', upstream, values_full)
    score_grad = softmax_out * (prob_grad - jnp.transpose(row_dot, (1, 2, 0))[..., None])
    score_grad = lax.optimization_barrier(score_grad.astype(jnp.bfloat16)).astype(jnp.float32)
    grad_query = (jnp.einsum('kgij,jkd->ikgd', score_grad, keys_full) * score_scale).astype(jnp.bfloat16)
    key_grad = jnp.einsum('kgij,ikgd->jkd', score_grad, query_full) * score_scale
    value_grad = jnp.einsum('kgij,ikgd->jkd', weights, upstream)
    key_grad = key_grad.reshape(key_count, KVH * HD)
    value_grad = value_grad.reshape(key_count, KVH * HD)
    prompt_grad = jnp.stack([key_grad[:PL], value_grad[:PL]]).astype(jnp.bfloat16)
    resp_key_grad = key_grad[PL:].astype(jnp.bfloat16)
    resp_value_grad = value_grad[PL:].astype(jnp.bfloat16)
    hidden_grad = jnp.dot(resp_key_grad, w_key.T, preferred_element_type=jnp.float32)
    hidden_grad = hidden_grad + jnp.dot(resp_value_grad, w_value.T, preferred_element_type=jnp.float32)
    return (grad_query.reshape(BT, HQ * HD), hidden_grad.astype(jnp.bfloat16), prompt_grad)

def reference(hidden, queries, out_grad, w_key, w_value, prompt_kv, block_dest, resp_len):
    nblocks = block_dest.shape[0]
    inputs = (hidden.reshape(nblocks, BT, D), queries.reshape(nblocks, BT, HQ * HD), out_grad.reshape(nblocks, BT, HQ * HD), prompt_kv[block_dest], resp_len)
    grad_query, hidden_grad, prompt_grad = lax.map(lambda block_in: one_block(block_in, w_key, w_value), inputs)
    grad_prompt = jax.ops.segment_sum(prompt_grad.astype(jnp.float32), block_dest, num_segments=nblocks)
    return (grad_query.reshape(nblocks * BT, HQ * HD), hidden_grad.reshape(nblocks * BT, D), grad_prompt.astype(jnp.bfloat16))
```

```python
import functools
import math

import jax
import jax.numpy as jnp
from jax import lax
from jax.experimental import pallas as pl
from jax.experimental.pallas import tpu as pltpu
from jax.sharding import PartitionSpec as P

HD = 128
GROUP = 4
HEADS_AT_ONCE = 2
X_BIT = 1
Y_BIT = 2

big_negative = -1e30


def swap_with(block, axis, bit):
    return lax.ppermute(block, axis, [(i, i ^ bit) for i in range(lax.axis_size(axis))])


def attention_grads_kernel(
    meta_ref,
    queries,
    upstreams,
    resp_kv,
    own_keys,
    own_values,
    x_keys,
    y_keys,
    x_values,
    y_values,
    *refs,
    first,
    heads,
    kv_heads,
    prompt_len,
    group_size,
    aliased,
):
    refs = refs[aliased:]
    outputs, refs = refs[:5], refs[5:]
    query, upstream, keys, values, keys_t, value_grad, key_grad = refs[:7]
    results, (load_sems, store_sems) = refs[7:12], refs[12:]
    mode = meta_ref[0]
    length = meta_ref[1]
    rows = resp_kv.shape[0]
    score_scale = 1.0 / math.sqrt(HD)
    prompt_part = slice(0, prompt_len)
    resp_part = slice(prompt_len, prompt_len + rows)
    group_cols = group_size * HD

    def columns(ref, index, width):
        return ref.at[:, pl.ds(index * width, width)]

    def loads(h):
        key_rows = keys.at[h, pl.ds(0, prompt_len)]
        value_rows = values.at[h, pl.ds(0, prompt_len)]
        key_sources = [
            (mode == 0, own_keys),
            (mode == X_BIT, x_keys),
            (mode >= Y_BIT, y_keys),
        ]
        value_sources = [
            (mode == 0, own_values),
            (mode == Y_BIT, y_values),
            ((mode == X_BIT) | (mode == X_BIT + Y_BIT), x_values),
        ]
        resp_keys = columns(resp_kv, first + h, HD)
        resp_values = columns(resp_kv, kv_heads + first + h, HD)
        return [
            [(flag, columns(ref, h, HD), key_rows) for flag, ref in key_sources],
            [(None, resp_keys, keys.at[h, pl.ds(prompt_len, rows)])],
            [(None, columns(queries, first + h, group_cols), query.at[h])],
            [(flag, columns(ref, h, HD), value_rows) for flag, ref in value_sources],
            [(None, resp_values, values.at[h, pl.ds(prompt_len, rows)])],
            [(None, columns(upstreams, first + h, group_cols), upstream.at[h])],
        ]

    for h in range(heads):
        for slot, choices in enumerate(loads(h)):
            for flag, source, target in choices:
                copy = pltpu.make_async_copy(source, target, load_sems.at[h, slot])
                if flag is None:
                    copy.start()
                else:
                    pl.when(flag)(copy.start)

    key_pos = lax.broadcasted_iota(jnp.int32, (rows, rows), 0)
    row_pos = lax.broadcasted_iota(jnp.int32, (rows, rows), 1)
    visible = (key_pos <= row_pos) & (key_pos < length)
    visible = jnp.concatenate([visible.astype(jnp.int32)] * HEADS_AT_ONCE, axis=1) > 0
    live = lax.broadcasted_iota(jnp.int32, (rows, HD), 0) < length
    live = jnp.concatenate([live.astype(jnp.int32)] * HEADS_AT_ONCE, axis=0) > 0
    nt = (((1,), (1,)), ((), ()))
    tiles = group_size // HEADS_AT_ONCE

    def tile_inputs(h, index):
        if index == 0:
            for slot, choices in enumerate(loads(h)):
                _, source, target = choices[0]
                pltpu.make_async_copy(source, target, load_sems.at[h, slot]).wait()
            keys_t[h] = keys[h].T
        parts = range(index * HEADS_AT_ONCE, (index + 1) * HEADS_AT_ONCE)
        parts = [slice(k * HD, (k + 1) * HD) for k in parts]
        tile_query = jnp.concatenate([query[h, :, part] for part in parts], axis=0)
        tile_upstream = jnp.concatenate([upstream[h, :, part] for part in parts], axis=0)
        tile_upstream = jnp.where(live, tile_upstream, jnp.zeros((), jnp.bfloat16))
        scores = lax.dot_general(keys[h], tile_query, nt, preferred_element_type=jnp.float32)
        prob_grad = lax.dot_general(
            values[h], tile_upstream, nt, preferred_element_type=jnp.float32
        )
        return parts, tile_query, tile_upstream, scores, prob_grad

    def store(h, slot, target):
        copy = pltpu.make_async_copy(results[slot].at[h], target, store_sems.at[h, slot])
        copy.start()
        return copy

    stores = []
    steps = [(h, index) for h in range(heads) for index in range(tiles)]
    following = tile_inputs(*steps[0])
    for step, (h, index) in enumerate(steps):
        parts, tile_query, tile_upstream, scores, prob_grad = following
        if step + 1 < len(steps):
            following = tile_inputs(*steps[step + 1])
        resp_scores = jnp.where(visible, scores[prompt_len:], big_negative)
        scores = jnp.concatenate([scores[:prompt_len], resp_scores], axis=0)
        peak = jnp.max(scores, axis=0, keepdims=True)
        exponent = jnp.exp2((scores - peak) * (score_scale * math.log2(math.e)))
        probs = exponent * (1.0 / jnp.sum(exponent, axis=0, keepdims=True))
        weights = probs.astype(jnp.bfloat16)
        row_dot = jnp.sum(weights.astype(jnp.float32) * prob_grad, axis=0, keepdims=True)
        score_grad = (probs * (prob_grad - row_dot)).astype(jnp.bfloat16)
        value_term = jnp.dot(weights, tile_upstream, preferred_element_type=jnp.float32)
        key_term = jnp.dot(score_grad, tile_query, preferred_element_type=jnp.float32)
        query_grad_t = jnp.dot(keys_t[h], score_grad, preferred_element_type=jnp.float32)
        query_grad = (query_grad_t * score_scale).T.astype(jnp.bfloat16)
        for k, part in enumerate(parts):
            results[0][h, :, part] = query_grad[k * rows : (k + 1) * rows]
        if index > 0:
            value_term = value_grad[...] + value_term
            key_term = key_grad[...] + key_term
        if index + 1 < tiles:
            value_grad[...] = value_term
            key_grad[...] = key_term
            continue
        value_term = value_term.astype(jnp.bfloat16)
        results[2][h] = value_term[resp_part]
        results[4][h] = value_term[prompt_part]
        key_term = (key_term * score_scale).astype(jnp.bfloat16)
        results[1][h] = key_term[resp_part]
        results[3][h] = key_term[prompt_part]
        stores += [
            store(h, 0, columns(outputs[0], first + h, group_cols)),
            store(h, 1, columns(outputs[1], first + h, HD)),
            store(h, 2, columns(outputs[2], first + h, HD)),
            store(h, 3, columns(outputs[3], h, HD)),
            store(h, 4, columns(outputs[4], h, HD)),
        ]
    for copy in stores:
        copy.wait()


def chunk_grads(first, heads, meta, queries, out_grad, resp_kv, sources, prompt_len, earlier):
    rows, query_cols = queries.shape
    kv_cols = resp_kv.shape[1] // 2
    group_size = query_cols // kv_cols
    group_cols = group_size * HD
    key_count = prompt_len + rows
    bf16 = jnp.bfloat16
    part = jax.ShapeDtypeStruct((prompt_len, heads * HD), bf16)
    matmul_flops = 2 * heads * group_size * rows * key_count * HD
    anywhere = pl.BlockSpec(memory_space=pl.ANY)
    return pl.pallas_call(
        functools.partial(
            attention_grads_kernel,
            first=first,
            heads=heads,
            kv_heads=kv_cols // HD,
            prompt_len=prompt_len,
            group_size=group_size,
            aliased=len(earlier),
        ),
        in_specs=[pl.BlockSpec(memory_space=pltpu.SMEM)] + [anywhere] * (9 + len(earlier)),
        out_specs=[anywhere] * 5,
        scratch_shapes=[
            pltpu.VMEM((heads, rows, group_cols), bf16),
            pltpu.VMEM((heads, rows, group_cols), bf16),
            pltpu.VMEM((heads, key_count, HD), bf16),
            pltpu.VMEM((heads, key_count, HD), bf16),
            pltpu.VMEM((heads, HD, key_count), bf16),
            pltpu.VMEM((key_count, HD), jnp.float32),
            pltpu.VMEM((key_count, HD), jnp.float32),
            pltpu.VMEM((heads, rows, group_cols), bf16),
            pltpu.VMEM((heads, rows, HD), bf16),
            pltpu.VMEM((heads, rows, HD), bf16),
            pltpu.VMEM((heads, prompt_len, HD), bf16),
            pltpu.VMEM((heads, prompt_len, HD), bf16),
            pltpu.SemaphoreType.DMA((heads, 6)),
            pltpu.SemaphoreType.DMA((heads, 5)),
        ],
        out_shape=[
            jax.ShapeDtypeStruct((rows, query_cols), bf16),
            jax.ShapeDtypeStruct((rows, kv_cols), bf16),
            jax.ShapeDtypeStruct((rows, kv_cols), bf16),
            part,
            part,
        ],
        input_output_aliases={10 + k: k for k in range(len(earlier))},
        compiler_params=pltpu.CompilerParams(vmem_limit_bytes=32 * 1024 * 1024),
        cost_estimate=pl.CostEstimate(
            flops=10 * matmul_flops,
            bytes_accessed=8 * heads * prompt_len * HD * 2,
            transcendentals=heads * group_size * rows * key_count,
        ),
        name="attention_grads",
    )(meta, queries, out_grad, resp_kv, *sources, *earlier)


def flags_kernel(flags_ref, x_ref, y_ref, held_ref):
    row = lax.broadcasted_iota(jnp.int32, held_ref.shape, 0)
    held = jnp.zeros(held_ref.shape, jnp.int32)
    for k in range(flags_ref.shape[0]):
        held = jnp.where(row == k, flags_ref[k], held)
    held_ref[...] = held


def flags_after(flags, from_x, from_y):
    held = pl.pallas_call(
        flags_kernel,
        in_specs=[pl.BlockSpec(memory_space=pltpu.SMEM)]
        + [pl.BlockSpec(memory_space=pl.ANY)] * 2,
        out_shape=jax.ShapeDtypeStruct((8, HD), jnp.int32),
        cost_estimate=pl.CostEstimate(flops=2 * 10**10, bytes_accessed=0, transcendentals=0),
        name="flags_after",
    )(jnp.stack(flags).astype(jnp.int32), from_x, from_y)
    return [held[k, 0] != 0 for k in range(len(flags))]


def pick(flag, one, other):
    return jnp.where(flag, one, other)


def chunk_heads(kv_heads):
    if kv_heads == 1:
        return [1]
    return [kv_heads // 2, kv_heads - kv_heads // 2]


def masked_sum(first_flag, first, second_flag, second):
    zero = jnp.zeros((), jnp.float32)
    return jnp.where(first_flag, first.astype(jnp.float32), zero) + jnp.where(
        second_flag, second.astype(jnp.float32), zero
    )


def whole_features(hidden):
    if lax.axis_size("tensor") != 2:
        return lax.all_gather(hidden, "tensor", axis=1, tiled=True)
    other = swap_with(hidden, "tensor", 1)
    is_first = lax.axis_index("tensor") == 0
    return jnp.concatenate(
        [pick(is_first, hidden, other), pick(is_first, other, hidden)], axis=1
    )


def summed_share(partial_sum, share_cols):
    if lax.axis_size("tensor") != 2:
        return lax.psum_scatter(
            partial_sum.astype(jnp.bfloat16), "tensor", scatter_dimension=1, tiled=True
        )
    is_first = lax.axis_index("tensor") == 0
    low, high = partial_sum[:, :share_cols], partial_sum[:, share_cols:]
    sent = pick(is_first, high, low).astype(jnp.bfloat16)
    received = swap_with(sent, "tensor", 1).astype(jnp.float32)
    return (pick(is_first, low, high) + received).astype(jnp.bfloat16)


def local(hidden, queries, out_grad, w_key, w_value, prompt_kv, block_dest, resp_len):
    own = lax.axis_index("dp")
    prompt_pair = prompt_kv[0]
    prompt_len, kv_cols = prompt_pair.shape[1:]
    heads_of = chunk_heads(kv_cols // HD)
    chunks = len(heads_of)
    starts = [sum(heads_of[:c]) for c in range(chunks)]
    spans = [slice(first * HD, (first + n) * HD) for first, n in zip(starts, heads_of)]
    x_peer, y_peer = own ^ X_BIT, own ^ Y_BIT
    dest, x_dest, y_dest = block_dest[own], block_dest[x_peer], block_dest[y_peer]
    meta = jnp.stack([dest ^ own, resp_len[own]]).astype(jnp.int32)

    own_keys, own_values = [], []
    remaining = prompt_pair
    for c in range(chunks):
        own_keys.append(remaining[0, :, spans[c]])
        own_values.append(remaining[1, :, spans[c]])
        remaining, _ = lax.optimization_barrier((remaining, (own_keys[c], own_values[c])))
    x_keys = [swap_with(part, "dp", X_BIT) for part in own_keys]
    y_values = [swap_with(part, "dp", Y_BIT) for part in own_values]

    full_hidden = whole_features(hidden)
    resp_kv = jnp.concatenate(
        [
            jnp.dot(full_hidden, w, preferred_element_type=jnp.float32).astype(jnp.bfloat16)
            for w in (w_key, w_value)
        ],
        axis=1,
    )

    x_values, y_keys = [], []
    held = (own_keys, own_values, x_keys, y_values)
    for c in range(chunks):
        keys, values, relay_keys, relay_values = (part[c] for part in held)
        sent = (pick(x_dest == own, values, relay_values), pick(y_dest == own, keys, relay_keys))
        x_values.append(swap_with(sent[0], "dp", X_BIT))
        y_keys.append(swap_with(sent[1], "dp", Y_BIT))
        held, _ = lax.optimization_barrier((held, sent))

    earlier = []
    key_parts, value_parts = [], []
    for c in range(chunks):
        sources = [own_keys[c], own_values[c], x_keys[c], y_keys[c], x_values[c], y_values[c]]
        *earlier, key_part, value_part = chunk_grads(
            starts[c], heads_of[c], meta, queries, out_grad, resp_kv, sources, prompt_len, earlier
        )
        key_parts.append(key_part)
        value_parts.append(value_part)
    grad_query, resp_key_grad, resp_value_grad = earlier

    flags = [dest == y_peer, x_dest == y_peer, dest == x_peer, y_dest == x_peer]
    grad_prompt = jnp.zeros(prompt_pair.shape, jnp.bfloat16)
    for c in range(chunks):
        from_x = swap_with(key_parts[c], "dp", X_BIT)
        from_y = swap_with(value_parts[c], "dp", Y_BIT)
        through_y = masked_sum(flags[0], key_parts[c], flags[1], from_x)
        through_x = masked_sum(flags[2], value_parts[c], flags[3], from_y)
        through_y, through_x = through_y.astype(jnp.bfloat16), through_x.astype(jnp.bfloat16)
        if c + 1 < chunks:
            flags = flags_after(flags, through_x, through_y)
        else:
            resp_key_grad, resp_value_grad, _ = lax.optimization_barrier(
                (resp_key_grad, resp_value_grad, (through_y, through_x))
            )
            partial_sum = jnp.einsum(
                "ic,dc->id", resp_key_grad, w_key, preferred_element_type=jnp.float32
            )
            partial_sum = partial_sum + jnp.einsum(
                "ic,dc->id", resp_value_grad, w_value, preferred_element_type=jnp.float32
            )
            grad_hidden = summed_share(partial_sum, hidden.shape[1])
        last_y = swap_with(through_y, "dp", Y_BIT)
        last_x = swap_with(through_x, "dp", X_BIT)
        key_sum = masked_sum(dest == own, key_parts[c], x_dest == own, from_x)
        value_sum = masked_sum(dest == own, value_parts[c], y_dest == own, from_y)
        key_sum = (key_sum + last_y.astype(jnp.float32)).astype(jnp.bfloat16)
        value_sum = (value_sum + last_x.astype(jnp.float32)).astype(jnp.bfloat16)
        at = starts[c] * HD
        grad_prompt = lax.dynamic_update_slice(grad_prompt, key_sum[None], (0, 0, at))
        grad_prompt = lax.dynamic_update_slice(grad_prompt, value_sum[None], (1, 0, at))
    return (grad_query, grad_hidden, grad_prompt[None])


def solution(mesh):
    return jax.shard_map(
        local,
        mesh=mesh,
        in_specs=(
            P("dp", "tensor"),
            P("dp", "tensor"),
            P("dp", "tensor"),
            P(None, "tensor"),
            P(None, "tensor"),
            P("dp", None, None, "tensor"),
            P(),
            P(),
        ),
        out_specs=(P("dp", "tensor"), P("dp", "tensor"), P("dp", None, None, "tensor")),
        check_vma=False,
    )
```

```python
import functools
import math

import jax
import jax.numpy as jnp
from jax import lax
from jax.experimental import pallas as pl
from jax.experimental.pallas import tpu as pltpu
from jax.sharding import PartitionSpec as P

HD = 128
GROUP = 4
HEADS_AT_ONCE = 2
STRIP = 384
X_BIT = 1
Y_BIT = 2

big_negative = -1e30


def swap_with(block, axis, bit):
    return lax.ppermute(block, axis, [(i, i ^ bit) for i in range(lax.axis_size(axis))])


def attention_grads_kernel(
    meta_ref,
    queries,
    upstreams,
    resp_kv,
    own_keys,
    own_values,
    x_keys,
    y_keys,
    x_values,
    y_values,
    *refs,
    first,
    heads,
    kv_heads,
    prompt_len,
    group_size,
    aliased,
):
    refs = refs[aliased:]
    outputs, refs = refs[:5], refs[5:]
    query, upstream, keys, values, keys_t, value_grad, key_grad = refs[:7]
    scores, prob_grad, weights, score_grad = refs[7:11]
    results, (load_sems, store_sems) = refs[11:16], refs[16:]
    mode = meta_ref[0]
    length = meta_ref[1]
    rows = resp_kv.shape[0]
    key_count = prompt_len + rows
    score_scale = 1.0 / math.sqrt(HD)
    prompt_part = slice(0, prompt_len)
    resp_part = slice(prompt_len, prompt_len + rows)
    group_cols = group_size * HD

    def columns(ref, index, width):
        return ref.at[:, pl.ds(index * width, width)]

    def loads(h):
        key_rows = keys.at[h, pl.ds(0, prompt_len)]
        value_rows = values.at[h, pl.ds(0, prompt_len)]
        key_sources = [
            (mode == 0, own_keys),
            (mode == X_BIT, x_keys),
            (mode >= Y_BIT, y_keys),
        ]
        value_sources = [
            (mode == 0, own_values),
            (mode == Y_BIT, y_values),
            ((mode == X_BIT) | (mode == X_BIT + Y_BIT), x_values),
        ]
        resp_keys = columns(resp_kv, first + h, HD)
        resp_values = columns(resp_kv, kv_heads + first + h, HD)
        return [
            [(flag, columns(ref, h, HD), key_rows) for flag, ref in key_sources],
            [(None, resp_keys, keys.at[h, pl.ds(prompt_len, rows)])],
            [(None, columns(queries, first + h, group_cols), query.at[h])],
            [(flag, columns(ref, h, HD), value_rows) for flag, ref in value_sources],
            [(None, resp_values, values.at[h, pl.ds(prompt_len, rows)])],
            [(None, columns(upstreams, first + h, group_cols), upstream.at[h])],
        ]

    for h in range(heads):
        for slot, choices in enumerate(loads(h)):
            for flag, source, target in choices:
                copy = pltpu.make_async_copy(source, target, load_sems.at[h, slot])
                if flag is None:
                    copy.start()
                else:
                    pl.when(flag)(copy.start)

    key_pos = lax.broadcasted_iota(jnp.int32, (rows, rows), 0)
    row_pos = lax.broadcasted_iota(jnp.int32, (rows, rows), 1)
    visible = (key_pos <= row_pos) & (key_pos < length)
    visible = jnp.concatenate([visible.astype(jnp.int32)] * HEADS_AT_ONCE, axis=1) > 0
    live = lax.broadcasted_iota(jnp.int32, (rows, HD), 0) < length
    live = jnp.concatenate([live.astype(jnp.int32)] * HEADS_AT_ONCE, axis=0) > 0
    nt = (((1,), (1,)), ((), ()))
    tiles = group_size // HEADS_AT_ONCE

    def tile_inputs(h, index):
        if index == 0:
            for slot, choices in enumerate(loads(h)):
                _, source, target = choices[0]
                pltpu.make_async_copy(source, target, load_sems.at[h, slot]).wait()
            keys_t[h] = keys[h].T
        parts = range(index * HEADS_AT_ONCE, (index + 1) * HEADS_AT_ONCE)
        parts = [slice(k * HD, (k + 1) * HD) for k in parts]
        tile_query = jnp.concatenate([query[h, :, part] for part in parts], axis=0)
        tile_upstream = jnp.concatenate([upstream[h, :, part] for part in parts], axis=0)
        tile_upstream = jnp.where(live, tile_upstream, jnp.zeros((), jnp.bfloat16))
        return h, parts, tile_query, tile_upstream

    def put_scores(buffer, tile, strip, peak):
        part = lax.dot_general(keys[tile[0], strip], tile[2], nt, preferred_element_type=jnp.float32)
        if strip.stop == key_count:
            resp_scores = jnp.where(visible, part[-rows:], big_negative)
            part = jnp.concatenate([part[:-rows], resp_scores], axis=0)
        scores[buffer, strip] = part
        part_peak = jnp.max(part, axis=0, keepdims=True)
        return part_peak if peak is None else jnp.maximum(peak, part_peak)

    def put_prob_grad(buffer, tile, strip):
        prob_grad[buffer, strip] = lax.dot_general(
            values[tile[0], strip], tile[3], nt, preferred_element_type=jnp.float32
        )

    def store(h, slot, target):
        copy = pltpu.make_async_copy(results[slot].at[h], target, store_sems.at[h, slot])
        copy.start()
        return copy

    stores = []
    strips = [slice(i, i + STRIP) for i in range(0, key_count, STRIP)]
    steps = [(h, index) for h in range(heads) for index in range(tiles)]
    following = tile_inputs(*steps[0])
    following_peak = None
    for strip in strips:
        following_peak = put_scores(0, following, strip, following_peak)
        put_prob_grad(0, following, strip)
    for step, (h, index) in enumerate(steps):
        now, later = step % 2, (step + 1) % 2
        (_, parts, tile_query, tile_upstream), peak = following, following_peak
        more = step + 1 < len(steps)
        if more:
            following, following_peak = tile_inputs(*steps[step + 1]), None
        total = jnp.zeros((1, scores.shape[2]), jnp.float32)
        for strip in strips:
            if more:
                following_peak = put_scores(later, following, strip, following_peak)
            exponent = (scores[now, strip] - peak) * (score_scale * math.log2(math.e))
            exponent = jnp.exp2(exponent)
            scores[now, strip] = exponent
            total += jnp.sum(exponent, axis=0, keepdims=True)
        inverse = 1.0 / total
        row_dot = jnp.zeros_like(total)
        for strip in strips:
            if more:
                put_prob_grad(later, following, strip)
            part = (scores[now, strip] * inverse).astype(jnp.bfloat16)
            weights[strip] = part
            part = part.astype(jnp.float32) * prob_grad[now, strip]
            row_dot += jnp.sum(part, axis=0, keepdims=True)
        for strip in strips:
            part = scores[now, strip] * inverse * (prob_grad[now, strip] - row_dot)
            part = part.astype(jnp.bfloat16)
            score_grad[strip] = part
            value_term = jnp.dot(weights[strip], tile_upstream, preferred_element_type=jnp.float32)
            key_term = jnp.dot(part, tile_query, preferred_element_type=jnp.float32)
            value_grad[strip] = value_grad[strip] + value_term if index > 0 else value_term
            key_grad[strip] = key_grad[strip] + key_term if index > 0 else key_term
        query_grad_t = jnp.dot(keys_t[h], score_grad[...], preferred_element_type=jnp.float32)
        query_grad = (query_grad_t * score_scale).T.astype(jnp.bfloat16)
        for k, part in enumerate(parts):
            results[0][h, :, part] = query_grad[k * rows : (k + 1) * rows]
        if index + 1 < tiles:
            continue
        value_term = value_grad[...].astype(jnp.bfloat16)
        results[2][h] = value_term[resp_part]
        results[4][h] = value_term[prompt_part]
        key_term = (key_grad[...] * score_scale).astype(jnp.bfloat16)
        results[1][h] = key_term[resp_part]
        results[3][h] = key_term[prompt_part]
        stores += [
            store(h, 0, columns(outputs[0], first + h, group_cols)),
            store(h, 1, columns(outputs[1], first + h, HD)),
            store(h, 2, columns(outputs[2], first + h, HD)),
            store(h, 3, columns(outputs[3], h, HD)),
            store(h, 4, columns(outputs[4], h, HD)),
        ]
    for copy in stores:
        copy.wait()


def chunk_grads(first, heads, meta, queries, out_grad, resp_kv, sources, prompt_len, earlier):
    rows, query_cols = queries.shape
    kv_cols = resp_kv.shape[1] // 2
    group_size = query_cols // kv_cols
    group_cols = group_size * HD
    key_count = prompt_len + rows
    bf16 = jnp.bfloat16
    part = jax.ShapeDtypeStruct((prompt_len, heads * HD), bf16)
    matmul_flops = 2 * heads * group_size * rows * key_count * HD
    anywhere = pl.BlockSpec(memory_space=pl.ANY)
    return pl.pallas_call(
        functools.partial(
            attention_grads_kernel,
            first=first,
            heads=heads,
            kv_heads=kv_cols // HD,
            prompt_len=prompt_len,
            group_size=group_size,
            aliased=len(earlier),
        ),
        in_specs=[pl.BlockSpec(memory_space=pltpu.SMEM)] + [anywhere] * (9 + len(earlier)),
        out_specs=[anywhere] * 5,
        scratch_shapes=[
            pltpu.VMEM((heads, rows, group_cols), bf16),
            pltpu.VMEM((heads, rows, group_cols), bf16),
            pltpu.VMEM((heads, key_count, HD), bf16),
            pltpu.VMEM((heads, key_count, HD), bf16),
            pltpu.VMEM((heads, HD, key_count), bf16),
            pltpu.VMEM((key_count, HD), jnp.float32),
            pltpu.VMEM((key_count, HD), jnp.float32),
            pltpu.VMEM((2, key_count, HEADS_AT_ONCE * rows), jnp.float32),
            pltpu.VMEM((2, key_count, HEADS_AT_ONCE * rows), jnp.float32),
            pltpu.VMEM((key_count, HEADS_AT_ONCE * rows), bf16),
            pltpu.VMEM((key_count, HEADS_AT_ONCE * rows), bf16),
            pltpu.VMEM((heads, rows, group_cols), bf16),
            pltpu.VMEM((heads, rows, HD), bf16),
            pltpu.VMEM((heads, rows, HD), bf16),
            pltpu.VMEM((heads, prompt_len, HD), bf16),
            pltpu.VMEM((heads, prompt_len, HD), bf16),
            pltpu.SemaphoreType.DMA((heads, 6)),
            pltpu.SemaphoreType.DMA((heads, 5)),
        ],
        out_shape=[
            jax.ShapeDtypeStruct((rows, query_cols), bf16),
            jax.ShapeDtypeStruct((rows, kv_cols), bf16),
            jax.ShapeDtypeStruct((rows, kv_cols), bf16),
            part,
            part,
        ],
        input_output_aliases={10 + k: k for k in range(len(earlier))},
        compiler_params=pltpu.CompilerParams(vmem_limit_bytes=32 * 1024 * 1024),
        cost_estimate=pl.CostEstimate(
            flops=10 * matmul_flops,
            bytes_accessed=8 * heads * prompt_len * HD * 2,
            transcendentals=heads * group_size * rows * key_count,
        ),
        name="attention_grads",
    )(meta, queries, out_grad, resp_kv, *sources, *earlier)


def flags_kernel(flags_ref, x_ref, y_ref, held_ref):
    row = lax.broadcasted_iota(jnp.int32, held_ref.shape, 0)
    held = jnp.zeros(held_ref.shape, jnp.int32)
    for k in range(flags_ref.shape[0]):
        held = jnp.where(row == k, flags_ref[k], held)
    held_ref[...] = held


def flags_after(flags, from_x, from_y):
    held = pl.pallas_call(
        flags_kernel,
        in_specs=[pl.BlockSpec(memory_space=pltpu.SMEM)]
        + [pl.BlockSpec(memory_space=pl.ANY)] * 2,
        out_shape=jax.ShapeDtypeStruct((8, HD), jnp.int32),
        cost_estimate=pl.CostEstimate(flops=2 * 10**10, bytes_accessed=0, transcendentals=0),
        name="flags_after",
    )(jnp.stack(flags).astype(jnp.int32), from_x, from_y)
    return [held[k, 0] != 0 for k in range(len(flags))]


def pick(flag, one, other):
    return jnp.where(flag, one, other)


def chunk_heads(kv_heads):
    if kv_heads == 1:
        return [1]
    return [kv_heads // 2, kv_heads - kv_heads // 2]


def masked_sum(first_flag, first, second_flag, second):
    zero = jnp.zeros((), jnp.float32)
    return jnp.where(first_flag, first.astype(jnp.float32), zero) + jnp.where(
        second_flag, second.astype(jnp.float32), zero
    )


def whole_features(hidden):
    if lax.axis_size("tensor") != 2:
        return lax.all_gather(hidden, "tensor", axis=1, tiled=True)
    other = swap_with(hidden, "tensor", 1)
    is_first = lax.axis_index("tensor") == 0
    return jnp.concatenate(
        [pick(is_first, hidden, other), pick(is_first, other, hidden)], axis=1
    )


def summed_share(partial_sum, share_cols):
    if lax.axis_size("tensor") != 2:
        return lax.psum_scatter(
            partial_sum.astype(jnp.bfloat16), "tensor", scatter_dimension=1, tiled=True
        )
    is_first = lax.axis_index("tensor") == 0
    low, high = partial_sum[:, :share_cols], partial_sum[:, share_cols:]
    sent = pick(is_first, high, low).astype(jnp.bfloat16)
    received = swap_with(sent, "tensor", 1).astype(jnp.float32)
    return (pick(is_first, low, high) + received).astype(jnp.bfloat16)


def local(hidden, queries, out_grad, w_key, w_value, prompt_kv, block_dest, resp_len):
    own = lax.axis_index("dp")
    prompt_pair = prompt_kv[0]
    prompt_len, kv_cols = prompt_pair.shape[1:]
    heads_of = chunk_heads(kv_cols // HD)
    chunks = len(heads_of)
    starts = [sum(heads_of[:c]) for c in range(chunks)]
    spans = [slice(first * HD, (first + n) * HD) for first, n in zip(starts, heads_of)]
    x_peer, y_peer = own ^ X_BIT, own ^ Y_BIT
    dest, x_dest, y_dest = block_dest[own], block_dest[x_peer], block_dest[y_peer]
    meta = jnp.stack([dest ^ own, resp_len[own]]).astype(jnp.int32)

    own_keys, own_values = [], []
    remaining = prompt_pair
    for c in range(chunks):
        own_keys.append(remaining[0, :, spans[c]])
        own_values.append(remaining[1, :, spans[c]])
        remaining, _ = lax.optimization_barrier((remaining, (own_keys[c], own_values[c])))
    x_keys = [swap_with(part, "dp", X_BIT) for part in own_keys]
    y_values = [swap_with(part, "dp", Y_BIT) for part in own_values]

    full_hidden = whole_features(hidden)
    resp_kv = jnp.concatenate(
        [
            jnp.dot(full_hidden, w, preferred_element_type=jnp.float32).astype(jnp.bfloat16)
            for w in (w_key, w_value)
        ],
        axis=1,
    )

    x_values, y_keys = [], []
    held = (own_keys, own_values, x_keys, y_values)
    for c in range(chunks):
        keys, values, relay_keys, relay_values = (part[c] for part in held)
        sent = (pick(x_dest == own, values, relay_values), pick(y_dest == own, keys, relay_keys))
        x_values.append(swap_with(sent[0], "dp", X_BIT))
        y_keys.append(swap_with(sent[1], "dp", Y_BIT))
        held, _ = lax.optimization_barrier((held, sent))

    earlier = []
    key_parts, value_parts = [], []
    for c in range(chunks):
        sources = [own_keys[c], own_values[c], x_keys[c], y_keys[c], x_values[c], y_values[c]]
        *earlier, key_part, value_part = chunk_grads(
            starts[c], heads_of[c], meta, queries, out_grad, resp_kv, sources, prompt_len, earlier
        )
        key_parts.append(key_part)
        value_parts.append(value_part)
    grad_query, resp_key_grad, resp_value_grad = earlier

    flags = [dest == y_peer, x_dest == y_peer, dest == x_peer, y_dest == x_peer]
    grad_prompt = jnp.zeros(prompt_pair.shape, jnp.bfloat16)
    for c in range(chunks):
        from_x = swap_with(key_parts[c], "dp", X_BIT)
        from_y = swap_with(value_parts[c], "dp", Y_BIT)
        through_y = masked_sum(flags[0], key_parts[c], flags[1], from_x)
        through_x = masked_sum(flags[2], value_parts[c], flags[3], from_y)
        through_y, through_x = through_y.astype(jnp.bfloat16), through_x.astype(jnp.bfloat16)
        if c + 1 < chunks:
            flags = flags_after(flags, through_x, through_y)
        else:
            resp_key_grad, resp_value_grad, _ = lax.optimization_barrier(
                (resp_key_grad, resp_value_grad, (through_y, through_x))
            )
            partial_sum = jnp.einsum(
                "ic,dc->id", resp_key_grad, w_key, preferred_element_type=jnp.float32
            )
            partial_sum = partial_sum + jnp.einsum(
                "ic,dc->id", resp_value_grad, w_value, preferred_element_type=jnp.float32
            )
            grad_hidden = summed_share(partial_sum, hidden.shape[1])
        last_y = swap_with(through_y, "dp", Y_BIT)
        last_x = swap_with(through_x, "dp", X_BIT)
        key_sum = masked_sum(dest == own, key_parts[c], x_dest == own, from_x)
        value_sum = masked_sum(dest == own, value_parts[c], y_dest == own, from_y)
        key_sum = (key_sum + last_y.astype(jnp.float32)).astype(jnp.bfloat16)
        value_sum = (value_sum + last_x.astype(jnp.float32)).astype(jnp.bfloat16)
        at = starts[c] * HD
        grad_prompt = lax.dynamic_update_slice(grad_prompt, key_sum[None], (0, 0, at))
        grad_prompt = lax.dynamic_update_slice(grad_prompt, value_sum[None], (1, 0, at))
    return (grad_query, grad_hidden, grad_prompt[None])


def solution(mesh):
    return jax.shard_map(
        local,
        mesh=mesh,
        in_specs=(
            P("dp", "tensor"),
            P("dp", "tensor"),
            P("dp", "tensor"),
            P(None, "tensor"),
            P(None, "tensor"),
            P("dp", None, None, "tensor"),
            P(),
            P(),
        ),
        out_specs=(P("dp", "tensor"), P("dp", "tensor"), P("dp", None, None, "tensor")),
        check_vma=False,
    )
```

```python
import functools
import math

import jax
import jax.numpy as jnp
from jax import lax
from jax.experimental import pallas as pl
from jax.experimental.pallas import tpu as pltpu
from jax.sharding import PartitionSpec as P

HD = 128
GROUP = 4
HEADS_AT_ONCE = 2
STRIP = 576
X_BIT = 1
Y_BIT = 2

big_negative = -1e30


def swap_with(block, axis, bit):
    return lax.ppermute(block, axis, [(i, i ^ bit) for i in range(lax.axis_size(axis))])


def attention_grads_kernel(
    meta_ref,
    queries,
    upstreams,
    resp_kv,
    own_keys,
    own_values,
    x_keys,
    y_keys,
    x_values,
    y_values,
    *refs,
    first,
    heads,
    kv_heads,
    prompt_len,
    group_size,
    aliased,
):
    refs = refs[aliased:]
    outputs, refs = refs[:5], refs[5:]
    query, upstream, keys, values, keys_t, value_grad, key_grad = refs[:7]
    scores, prob_grad, weights, score_grad = refs[7:11]
    results, (load_sems, store_sems) = refs[11:16], refs[16:]
    mode = meta_ref[0]
    length = meta_ref[1]
    rows = resp_kv.shape[0]
    key_count = prompt_len + rows
    score_scale = 1.0 / math.sqrt(HD)
    prompt_part = slice(0, prompt_len)
    resp_part = slice(prompt_len, prompt_len + rows)
    group_cols = group_size * HD

    def columns(ref, index, width):
        return ref.at[:, pl.ds(index * width, width)]

    def loads(h):
        key_rows = keys.at[h, pl.ds(0, prompt_len)]
        value_rows = values.at[h, pl.ds(0, prompt_len)]
        key_sources = [
            (mode == 0, own_keys),
            (mode == X_BIT, x_keys),
            (mode >= Y_BIT, y_keys),
        ]
        value_sources = [
            (mode == 0, own_values),
            (mode == Y_BIT, y_values),
            ((mode == X_BIT) | (mode == X_BIT + Y_BIT), x_values),
        ]
        resp_keys = columns(resp_kv, first + h, HD)
        resp_values = columns(resp_kv, kv_heads + first + h, HD)
        return [
            [(flag, columns(ref, h, HD), key_rows) for flag, ref in key_sources],
            [(None, resp_keys, keys.at[h, pl.ds(prompt_len, rows)])],
            [(None, columns(queries, first + h, group_cols), query.at[h])],
            [(flag, columns(ref, h, HD), value_rows) for flag, ref in value_sources],
            [(None, resp_values, values.at[h, pl.ds(prompt_len, rows)])],
            [(None, columns(upstreams, first + h, group_cols), upstream.at[h])],
        ]

    for h in range(heads):
        for slot, choices in enumerate(loads(h)):
            for flag, source, target in choices:
                copy = pltpu.make_async_copy(source, target, load_sems.at[h, slot])
                if flag is None:
                    copy.start()
                else:
                    pl.when(flag)(copy.start)

    key_pos = lax.broadcasted_iota(jnp.int32, (rows, rows), 0)
    row_pos = lax.broadcasted_iota(jnp.int32, (rows, rows), 1)
    visible = (key_pos <= row_pos) & (key_pos < length)
    visible = jnp.concatenate([visible.astype(jnp.int32)] * HEADS_AT_ONCE, axis=1) > 0
    live = lax.broadcasted_iota(jnp.int32, (rows, HD), 0) < length
    live = jnp.concatenate([live.astype(jnp.int32)] * HEADS_AT_ONCE, axis=0) > 0
    nt = (((1,), (1,)), ((), ()))
    tiles = group_size // HEADS_AT_ONCE

    def tile_inputs(h, index):
        if index == 0:
            for slot, choices in enumerate(loads(h)):
                _, source, target = choices[0]
                pltpu.make_async_copy(source, target, load_sems.at[h, slot]).wait()
            keys_t[h] = keys[h].T
        parts = range(index * HEADS_AT_ONCE, (index + 1) * HEADS_AT_ONCE)
        parts = [slice(k * HD, (k + 1) * HD) for k in parts]
        tile_query = jnp.concatenate([query[h, :, part] for part in parts], axis=0)
        tile_upstream = jnp.concatenate([upstream[h, :, part] for part in parts], axis=0)
        tile_upstream = jnp.where(live, tile_upstream, jnp.zeros((), jnp.bfloat16))
        return h, parts, tile_query, tile_upstream

    def put_scores(buffer, tile, strip, peak):
        part = lax.dot_general(keys[tile[0], strip], tile[2], nt, preferred_element_type=jnp.float32)
        if strip.stop == key_count:
            resp_scores = jnp.where(visible, part[-rows:], big_negative)
            part = jnp.concatenate([part[:-rows], resp_scores], axis=0)
        scores[buffer, strip] = part
        part_peak = jnp.max(part, axis=0, keepdims=True)
        return part_peak if peak is None else jnp.maximum(peak, part_peak)

    def put_prob_grad(buffer, tile, strip):
        prob_grad[buffer, strip] = lax.dot_general(
            values[tile[0], strip], tile[3], nt, preferred_element_type=jnp.float32
        )

    def store(h, slot, target):
        copy = pltpu.make_async_copy(results[slot].at[h], target, store_sems.at[h, slot])
        copy.start()
        return copy

    stores = []
    strips = [slice(i, i + STRIP) for i in range(0, key_count, STRIP)]
    steps = [(h, index) for h in range(heads) for index in range(tiles)]
    following = tile_inputs(*steps[0])
    following_peak = None
    for strip in strips:
        following_peak = put_scores(0, following, strip, following_peak)
        put_prob_grad(0, following, strip)
    for step, (h, index) in enumerate(steps):
        now, later = step % 2, (step + 1) % 2
        (_, parts, tile_query, tile_upstream), peak = following, following_peak
        more = step + 1 < len(steps)
        if more:
            following, following_peak = tile_inputs(*steps[step + 1]), None
        total = jnp.zeros((1, scores.shape[2]), jnp.float32)
        for strip in strips:
            if more:
                following_peak = put_scores(later, following, strip, following_peak)
            exponent = (scores[now, strip] - peak) * (score_scale * math.log2(math.e))
            exponent = jnp.exp2(exponent)
            scores[now, strip] = exponent
            total += jnp.sum(exponent, axis=0, keepdims=True)
        inverse = 1.0 / total
        row_dot = jnp.zeros_like(total)
        for strip in strips:
            if more:
                put_prob_grad(later, following, strip)
            part = (scores[now, strip] * inverse).astype(jnp.bfloat16)
            weights[strip] = part
            part = part.astype(jnp.float32) * prob_grad[now, strip]
            row_dot += jnp.sum(part, axis=0, keepdims=True)
        for strip in strips:
            part = scores[now, strip] * inverse * (prob_grad[now, strip] - row_dot)
            part = part.astype(jnp.bfloat16)
            score_grad[strip] = part
            value_term = jnp.dot(weights[strip], tile_upstream, preferred_element_type=jnp.float32)
            key_term = jnp.dot(part, tile_query, preferred_element_type=jnp.float32)
            value_grad[strip] = value_grad[strip] + value_term if index > 0 else value_term
            key_grad[strip] = key_grad[strip] + key_term if index > 0 else key_term
        query_grad_t = jnp.dot(keys_t[h], score_grad[...], preferred_element_type=jnp.float32)
        query_grad = (query_grad_t * score_scale).T.astype(jnp.bfloat16)
        for k, part in enumerate(parts):
            results[0][h, :, part] = query_grad[k * rows : (k + 1) * rows]
        if index + 1 < tiles:
            continue
        value_term = value_grad[...].astype(jnp.bfloat16)
        results[2][h] = value_term[resp_part]
        results[4][h] = value_term[prompt_part]
        key_term = (key_grad[...] * score_scale).astype(jnp.bfloat16)
        results[1][h] = key_term[resp_part]
        results[3][h] = key_term[prompt_part]
        stores += [
            store(h, 0, columns(outputs[0], first + h, group_cols)),
            store(h, 1, columns(outputs[1], first + h, HD)),
            store(h, 2, columns(outputs[2], first + h, HD)),
            store(h, 3, columns(outputs[3], h, HD)),
            store(h, 4, columns(outputs[4], h, HD)),
        ]
    for copy in stores:
        copy.wait()


def chunk_grads(first, heads, meta, queries, out_grad, resp_kv, sources, prompt_len, earlier):
    rows, query_cols = queries.shape
    kv_cols = resp_kv.shape[1] // 2
    group_size = query_cols // kv_cols
    group_cols = group_size * HD
    key_count = prompt_len + rows
    bf16 = jnp.bfloat16
    part = jax.ShapeDtypeStruct((prompt_len, heads * HD), bf16)
    matmul_flops = 2 * heads * group_size * rows * key_count * HD
    anywhere = pl.BlockSpec(memory_space=pl.ANY)
    return pl.pallas_call(
        functools.partial(
            attention_grads_kernel,
            first=first,
            heads=heads,
            kv_heads=kv_cols // HD,
            prompt_len=prompt_len,
            group_size=group_size,
            aliased=len(earlier),
        ),
        in_specs=[pl.BlockSpec(memory_space=pltpu.SMEM)] + [anywhere] * (9 + len(earlier)),
        out_specs=[anywhere] * 5,
        scratch_shapes=[
            pltpu.VMEM((heads, rows, group_cols), bf16),
            pltpu.VMEM((heads, rows, group_cols), bf16),
            pltpu.VMEM((heads, key_count, HD), bf16),
            pltpu.VMEM((heads, key_count, HD), bf16),
            pltpu.VMEM((heads, HD, key_count), bf16),
            pltpu.VMEM((key_count, HD), jnp.float32),
            pltpu.VMEM((key_count, HD), jnp.float32),
            pltpu.VMEM((2, key_count, HEADS_AT_ONCE * rows), jnp.float32),
            pltpu.VMEM((2, key_count, HEADS_AT_ONCE * rows), jnp.float32),
            pltpu.VMEM((key_count, HEADS_AT_ONCE * rows), bf16),
            pltpu.VMEM((key_count, HEADS_AT_ONCE * rows), bf16),
            pltpu.VMEM((heads, rows, group_cols), bf16),
            pltpu.VMEM((heads, rows, HD), bf16),
            pltpu.VMEM((heads, rows, HD), bf16),
            pltpu.VMEM((heads, prompt_len, HD), bf16),
            pltpu.VMEM((heads, prompt_len, HD), bf16),
            pltpu.SemaphoreType.DMA((heads, 6)),
            pltpu.SemaphoreType.DMA((heads, 5)),
        ],
        out_shape=[
            jax.ShapeDtypeStruct((rows, query_cols), bf16),
            jax.ShapeDtypeStruct((rows, kv_cols), bf16),
            jax.ShapeDtypeStruct((rows, kv_cols), bf16),
            part,
            part,
        ],
        input_output_aliases={10 + k: k for k in range(len(earlier))},
        compiler_params=pltpu.CompilerParams(vmem_limit_bytes=32 * 1024 * 1024),
        cost_estimate=pl.CostEstimate(
            flops=10 * matmul_flops,
            bytes_accessed=8 * heads * prompt_len * HD * 2,
            transcendentals=heads * group_size * rows * key_count,
        ),
        name="attention_grads",
    )(meta, queries, out_grad, resp_kv, *sources, *earlier)


def flags_kernel(flags_ref, x_ref, y_ref, held_ref):
    row = lax.broadcasted_iota(jnp.int32, held_ref.shape, 0)
    held = jnp.zeros(held_ref.shape, jnp.int32)
    for k in range(flags_ref.shape[0]):
        held = jnp.where(row == k, flags_ref[k], held)
    held_ref[...] = held


def flags_after(flags, from_x, from_y):
    held = pl.pallas_call(
        flags_kernel,
        in_specs=[pl.BlockSpec(memory_space=pltpu.SMEM)]
        + [pl.BlockSpec(memory_space=pl.ANY)] * 2,
        out_shape=jax.ShapeDtypeStruct((8, HD), jnp.int32),
        cost_estimate=pl.CostEstimate(flops=2 * 10**10, bytes_accessed=0, transcendentals=0),
        name="flags_after",
    )(jnp.stack(flags).astype(jnp.int32), from_x, from_y)
    return [held[k, 0] != 0 for k in range(len(flags))]


def pick(flag, one, other):
    return jnp.where(flag, one, other)


def chunk_heads(kv_heads):
    if kv_heads == 1:
        return [1]
    return [kv_heads // 2, kv_heads - kv_heads // 2]


def masked_sum(first_flag, first, second_flag, second):
    zero = jnp.zeros((), jnp.float32)
    return jnp.where(first_flag, first.astype(jnp.float32), zero) + jnp.where(
        second_flag, second.astype(jnp.float32), zero
    )


def whole_features(hidden):
    if lax.axis_size("tensor") != 2:
        return lax.all_gather(hidden, "tensor", axis=1, tiled=True)
    other = swap_with(hidden, "tensor", 1)
    is_first = lax.axis_index("tensor") == 0
    return jnp.concatenate(
        [pick(is_first, hidden, other), pick(is_first, other, hidden)], axis=1
    )


def summed_share(partial_sum, share_cols):
    if lax.axis_size("tensor") != 2:
        return lax.psum_scatter(
            partial_sum.astype(jnp.bfloat16), "tensor", scatter_dimension=1, tiled=True
        )
    is_first = lax.axis_index("tensor") == 0
    low, high = partial_sum[:, :share_cols], partial_sum[:, share_cols:]
    sent = pick(is_first, high, low).astype(jnp.bfloat16)
    received = swap_with(sent, "tensor", 1).astype(jnp.float32)
    return (pick(is_first, low, high) + received).astype(jnp.bfloat16)


def local(hidden, queries, out_grad, w_key, w_value, prompt_kv, block_dest, resp_len):
    own = lax.axis_index("dp")
    prompt_pair = prompt_kv[0]
    prompt_len, kv_cols = prompt_pair.shape[1:]
    heads_of = chunk_heads(kv_cols // HD)
    chunks = len(heads_of)
    starts = [sum(heads_of[:c]) for c in range(chunks)]
    spans = [slice(first * HD, (first + n) * HD) for first, n in zip(starts, heads_of)]
    x_peer, y_peer = own ^ X_BIT, own ^ Y_BIT
    dest, x_dest, y_dest = block_dest[own], block_dest[x_peer], block_dest[y_peer]
    meta = jnp.stack([dest ^ own, resp_len[own]]).astype(jnp.int32)

    own_keys, own_values = [], []
    remaining = prompt_pair
    for c in range(chunks):
        own_keys.append(remaining[0, :, spans[c]])
        own_values.append(remaining[1, :, spans[c]])
        remaining, _ = lax.optimization_barrier((remaining, (own_keys[c], own_values[c])))
    x_keys = [swap_with(part, "dp", X_BIT) for part in own_keys]
    y_values = [swap_with(part, "dp", Y_BIT) for part in own_values]

    full_hidden = whole_features(hidden)
    resp_kv = jnp.concatenate(
        [
            jnp.dot(full_hidden, w, preferred_element_type=jnp.float32).astype(jnp.bfloat16)
            for w in (w_key, w_value)
        ],
        axis=1,
    )

    x_values, y_keys = [], []
    held = (own_keys, own_values, x_keys, y_values)
    for c in range(chunks):
        keys, values, relay_keys, relay_values = (part[c] for part in held)
        sent = (pick(x_dest == own, values, relay_values), pick(y_dest == own, keys, relay_keys))
        x_values.append(swap_with(sent[0], "dp", X_BIT))
        y_keys.append(swap_with(sent[1], "dp", Y_BIT))
        held, _ = lax.optimization_barrier((held, sent))

    earlier = []
    key_parts, value_parts = [], []
    for c in range(chunks):
        sources = [own_keys[c], own_values[c], x_keys[c], y_keys[c], x_values[c], y_values[c]]
        *earlier, key_part, value_part = chunk_grads(
            starts[c], heads_of[c], meta, queries, out_grad, resp_kv, sources, prompt_len, earlier
        )
        key_parts.append(key_part)
        value_parts.append(value_part)
    grad_query, resp_key_grad, resp_value_grad = earlier

    flags = [dest == y_peer, x_dest == y_peer, dest == x_peer, y_dest == x_peer]
    grad_prompt = jnp.zeros(prompt_pair.shape, jnp.bfloat16)
    for c in range(chunks):
        from_x = swap_with(key_parts[c], "dp", X_BIT)
        from_y = swap_with(value_parts[c], "dp", Y_BIT)
        through_y = masked_sum(flags[0], key_parts[c], flags[1], from_x)
        through_x = masked_sum(flags[2], value_parts[c], flags[3], from_y)
        through_y, through_x = through_y.astype(jnp.bfloat16), through_x.astype(jnp.bfloat16)
        if c + 1 < chunks:
            flags = flags_after(flags, through_x, through_y)
        else:
            resp_key_grad, resp_value_grad, _ = lax.optimization_barrier(
                (resp_key_grad, resp_value_grad, (through_y, through_x))
            )
            partial_sum = jnp.einsum(
                "ic,dc->id", resp_key_grad, w_key, preferred_element_type=jnp.float32
            )
            partial_sum = partial_sum + jnp.einsum(
                "ic,dc->id", resp_value_grad, w_value, preferred_element_type=jnp.float32
            )
            grad_hidden = summed_share(partial_sum, hidden.shape[1])
        last_y = swap_with(through_y, "dp", Y_BIT)
        last_x = swap_with(through_x, "dp", X_BIT)
        key_sum = masked_sum(dest == own, key_parts[c], x_dest == own, from_x)
        value_sum = masked_sum(dest == own, value_parts[c], y_dest == own, from_y)
        key_sum = (key_sum + last_y.astype(jnp.float32)).astype(jnp.bfloat16)
        value_sum = (value_sum + last_x.astype(jnp.float32)).astype(jnp.bfloat16)
        at = starts[c] * HD
        grad_prompt = lax.dynamic_update_slice(grad_prompt, key_sum[None], (0, 0, at))
        grad_prompt = lax.dynamic_update_slice(grad_prompt, value_sum[None], (1, 0, at))
    return (grad_query, grad_hidden, grad_prompt[None])


def solution(mesh):
    return jax.shard_map(
        local,
        mesh=mesh,
        in_specs=(
            P("dp", "tensor"),
            P("dp", "tensor"),
            P("dp", "tensor"),
            P(None, "tensor"),
            P(None, "tensor"),
            P("dp", None, None, "tensor"),
            P(),
            P(),
        ),
        out_specs=(P("dp", "tensor"), P("dp", "tensor"), P("dp", None, None, "tensor")),
        check_vma=False,
    )
```
